32 devices in a mesh: pipe: 4 (over z), dp: 8 (over y, x, core).
Axes of the slice: x: 2, y: 2, z: 4, core: 2. Of those that a mesh axis runs over, the one named last changes fastest.
Arguments:
- images: bfloat16 [128, 14, 14, 384], P('dp'), may hold values from -6 to 6
- depth_kernel: float32 [7, 7, 384], replicated, may hold values from -0.875 to 0.875
- depth_bias: float32 [384], replicated, may hold values from -3 to 3
- norm_gain: float32 [384], replicated, may hold values from 0.1 to 1.9
- norm_shift: float32 [384], replicated, may hold values from -2 to 2
- up_weight: bfloat16 [384, 1536], replicated, may hold values from -0.3125 to 0.3125
- up_bias: float32 [1536], replicated, may hold values from -2 to 2
- down_weight: bfloat16 [1536, 384], replicated, may hold values from -0.15625 to 0.15625
- down_bias: float32 [384], replicated, may hold values from -2 to 2
- layer_scale: float32 [384], replicated, may hold values from 0.5 to 1.5
- merge_gain: float32 [384], replicated, may hold values from 0.1 to 1.9
- merge_shift: float32 [384], replicated, may hold values from -2 to 2
- patch_weight: bfloat16 [1536, 768], replicated, may hold values from -0.15625 to 0.15625
- patch_bias: float32 [768], replicated, may hold values from -2 to 2
- keep_mask: int32 [128], P('dp'), may hold values 0 or 1
- out_grad: bfloat16 [128, 7, 7, 768], P('dp'), may hold values from -6 to 6
Outputs:
- merged_maps: bfloat16 [128, 7, 7, 768], P('dp', None, None, 'pipe')
- image_grad: float32 [128, 14, 14, 384], P('dp', None, None, 'pipe')
- depth_kernel_grad: float32 [7, 7, 384], replicated
- depth_bias_grad: float32 [384], replicated
- norm_gain_grad: float32 [384], replicated
- norm_shift_grad: float32 [384], replicated
- up_weight_grad: float32 [384, 1536], replicated
- up_bias_grad: float32 [1536], replicated
- down_weight_grad: float32 [1536, 384], replicated
- down_bias_grad: float32 [384], replicated
- layer_scale_grad: float32 [384], replicated
- merge_gain_grad: float32 [384], replicated
- merge_shift_grad: float32 [384], replicated
- patch_weight_grad: float32 [1536, 768], replicated
- patch_bias_grad: float32 [768], replicated
The draws below stay inside these ranges and needn't reach their ends.
All inputs are finite; a program needn't handle non-finite values. No bound on the sum of `keep_mask` on one device may be relied on, other than what follows from the above.
Results may differ from the reference program's by a relative error of at most 0.0086.
Values may be sent and summed in bfloat16 or wider, within the bound.
A program may use at most 320 MiB of HBM per device.

```python
import jax
import jax.numpy as jnp
from jax import lax

C = 384
FF = 1536
OUT = 768
SIDE = 14
HALF = 7
GROUP = 16
IMAGES = 128
N_DP = 8


def set_ends(drawn, key, low, top_value):
    place = [jax.random.randint(jax.random.fold_in(key, axis), (), 0, length) for axis, length in enumerate(drawn.shape)]
    longest = drawn.shape.index(max(drawn.shape))
    next_to = place[:longest] + [(place[longest] + 1) % drawn.shape[longest]] + place[longest + 1:]
    return drawn.at[tuple(place)].set(low).at[tuple(next_to)].set(top_value)


def shard_levels(stream_key, dims, cuts, smallest, largest):
    factor_of = 1.0
    for dim, parts in cuts:
        heights = jax.random.uniform(jax.random.fold_in(jax.random.fold_in(stream_key, 6), dim), (parts,), jnp.float32, smallest / len(cuts), largest / len(cuts))
        factor_of = factor_of * jnp.repeat(jnp.exp(heights), dims[dim] // parts).reshape((-1,) + (1,) * (len(dims) - 1 - dim))
    return factor_of


def normal_values(rng, extent, spread, reach, cuts=(), kind=jnp.bfloat16):
    drawn = jax.random.normal(rng, extent, jnp.float32) * spread
    if len(cuts) > 0:
        drawn = shard_levels(rng, extent, cuts, -0.22, 0.18) * drawn
    return jnp.clip(drawn, min=-reach, max=reach).astype(kind)


def setup_inputs(seed: int = 0) -> dict:
    arg_keys = jax.random.split(jax.random.key(seed), 17)
    return {
        "images": normal_values(arg_keys[0], (IMAGES, SIDE, SIDE, C), 1.0, 6.0, ((0, 8),)),
        "depth_kernel": normal_values(arg_keys[1], (7, 7, C), 49 ** -0.5, 0.875, (), jnp.float32),
        "depth_bias": normal_values(arg_keys[2], (C,), 0.5, 3.0, (), jnp.float32),
        "norm_gain": jnp.clip(1.0 + 0.18 * jax.random.normal(arg_keys[3], (C,), jnp.float32), 0.1, 1.9),
        "norm_shift": normal_values(arg_keys[4], (C,), 0.3, 2.0, (), jnp.float32),
        "up_weight": normal_values(arg_keys[5], (C, FF), C ** -0.5, 0.3125),
        "up_bias": normal_values(arg_keys[6], (FF,), 0.3, 2.0, (), jnp.float32),
        "down_weight": normal_values(arg_keys[7], (FF, C), FF ** -0.5, 0.15625),
        "down_bias": normal_values(arg_keys[8], (C,), 0.3, 2.0, (), jnp.float32),
        "layer_scale": jnp.clip(jax.random.uniform(arg_keys[9], (C,), jnp.float32, 0.5, 1.5), 0.5, 1.5),
        "merge_gain": jnp.clip(1.0 + 0.18 * jax.random.normal(arg_keys[10], (C,), jnp.float32), 0.1, 1.9),
        "merge_shift": normal_values(arg_keys[11], (C,), 0.3, 2.0, (), jnp.float32),
        "patch_weight": normal_values(arg_keys[12], (4 * C, OUT), (4 * C) ** -0.5, 0.15625),
        "patch_bias": normal_values(arg_keys[13], (OUT,), 0.3, 2.0, (), jnp.float32),
        "keep_mask": set_ends((jax.random.randint(arg_keys[14], (IMAGES,), 0, 10) < 9).astype(jnp.int32), jax.random.fold_in(arg_keys[14], 1), 0, 1),
        "out_grad": normal_values(arg_keys[15], (IMAGES, HALF, HALF, OUT), 1.0, 6.0, ((0, 8),)),
    }


@jax.custom_vjp
def low(v):
    return lax.optimization_barrier(v.astype(jnp.bfloat16)).astype(jnp.float32)

@jax.custom_vjp
def low_back(v):
    return v

def low_keep(v):
    return (low(v), None)

def low_pass(kept, grad):
    return (grad,)

def back_keep(v):
    return (v, None)

def back_low(kept, grad):
    return (low(grad),)
low.defvjp(low_keep, low_pass)
low_back.defvjp(back_keep, back_low)

def layer_norm(values, gain, shift):
    mean = lax.optimization_barrier(jnp.mean(values, axis=-1, keepdims=True))
    centered = values - mean
    variance = lax.optimization_barrier(jnp.mean(centered * centered, axis=-1, keepdims=True))
    return centered * lax.rsqrt(variance + 1e-06) * gain + shift

def depthwise(inputs, kernel, bias):
    height = inputs.shape[1]
    width = inputs.shape[2]
    padded = jnp.pad(inputs, ((0, 0), (3, 3), (3, 3), (0, 0)))
    total = bias + jnp.zeros_like(inputs)
    for across in range(7):
        for down in range(7):
            total = total + padded[:, across:across + height, down:down + width, :] * kernel[across, down]
    return total

def forward(params, inputs, keep):
    kernel, kbias, gain_one, shift_one, wup, bup, wdown, bdown, scale_gain, gain_two, shift_two, wpatch, bpatch = params
    highest = lax.Precision.HIGHEST
    normed = low_back(low(layer_norm(depthwise(inputs, kernel, kbias), gain_one, shift_one)))
    hidden = low_back(jnp.einsum('nhwc,cf->nhwf', normed, wup, precision=highest) + bup)
    activated = low_back(low(jax.nn.gelu(hidden, approximate=False)))
    branch = low_back(jnp.einsum('nhwf,fc->nhwc', activated, wdown, precision=highest) + bdown)
    factor = (keep.astype(jnp.float32) / 0.9)[:, None, None, None]
    residual = low_back(low(inputs + factor * scale_gain * branch))
    merge_in = low(layer_norm(residual, gain_two, shift_two))
    count, height, width, chans = merge_in.shape
    patches = merge_in.reshape(count, height // 2, 2, width // 2, 2, chans)
    patches = patches.transpose(0, 1, 3, 2, 4, 5).reshape(count, height // 2, width // 2, 4 * chans)
    return jnp.einsum('nhwk,ko->nhwo', patches, wpatch, precision=highest) + bpatch

def reference(images, depth_kernel, depth_bias, norm_gain, norm_shift, up_weight, up_bias, down_weight, down_bias, layer_scale, merge_gain, merge_shift, patch_weight, patch_bias, keep_mask, out_grad):
    params = tuple((item.astype(jnp.float32) for item in (depth_kernel, depth_bias, norm_gain, norm_shift, up_weight, up_bias, down_weight, down_bias, layer_scale, merge_gain, merge_shift, patch_weight, patch_bias)))
    stacks = (images.reshape((N_DP, GROUP) + images.shape[1:]), keep_mask.reshape(N_DP, GROUP), out_grad.reshape((N_DP, GROUP) + out_grad.shape[1:]))

    def block_step(carry, pieces):
        block_images, block_keep, block_grad = pieces
        outputs, pull = jax.vjp(lambda prm, inputs: forward(prm, inputs, block_keep), params, block_images.astype(jnp.float32))
        param_grads, input_grads = pull(block_grad.astype(jnp.float32))
        carry = tuple((total + part for total, part in zip(carry, param_grads)))
        return (carry, (outputs.astype(jnp.bfloat16), input_grads))
    initial = tuple((jnp.zeros(item.shape, jnp.float32) for item in params))
    totals, (maps, input_all) = lax.scan(block_step, initial, stacks)
    merged = maps.reshape(IMAGES, HALF, HALF, OUT)
    image_grad = input_all.reshape(IMAGES, SIDE, SIDE, C)
    return (merged, image_grad, totals[0], totals[1], totals[2], totals[3], totals[4], totals[5], totals[6], totals[7], totals[8], totals[9], totals[10], totals[11], totals[12])
```

```python
import functools
from types import SimpleNamespace

import jax
import jax.numpy as jnp
import numpy as np
from jax import lax
from jax.experimental import pallas as pl
from jax.experimental.pallas import tpu as pltpu
from jax.sharding import PartitionSpec as P

C = 384
FF = 1536
OUT = 768
SIDE = 14
WIDE = 16
HALF = 7
RING = SIDE + 3
FREQ = 160
SPEC = 2 * FREQ
MAP = SIDE * WIDE
CELLS = HALF * 8
TAPS = 56
SMALL = 64
F32 = jnp.float32
BF16 = jnp.bfloat16


def split_matrix(matrix):
    high = matrix.astype(BF16)
    low = (matrix - high.astype(np.float64)).astype(BF16)
    return high, low


def transforms():
    pairs = [(0, 0)] + [(u, 0) for u in range(1, 9)] + [(u, v) for v in range(1, 9) for u in range(RING)]
    freq = np.zeros((FREQ, 2))
    freq[: len(pairs)] = np.array(pairs)
    live = (np.arange(FREQ) < len(pairs)).astype(np.float64)
    weight = np.where(np.arange(FREQ) == 0, 1.0, 2.0) * live
    plain = np.array([(h, w, w < SIDE) for h in range(SIDE) for w in range(WIDE)])
    cell = np.array(
        [(h, 2 * b + j, b < HALF) for h in range(SIDE) for j in range(2) for b in range(8)]
    )
    taps = np.array([(i - 3, j - 3, j < 7) for i in range(7) for j in range(8)])

    def angles(places):
        return 2 * np.pi / RING * (freq @ places[:, :2].T)

    def forward(places, sign):
        turn = angles(places)
        scale = places[:, 2][None, :] * live[:, None] / RING
        return np.concatenate([np.cos(turn) * scale, sign * np.sin(turn) * scale], 0)

    def backward(places):
        turn = angles(places).T
        scale = places[:, 2][:, None] * weight[None, :] / RING
        return np.concatenate([np.cos(turn) * scale, -np.sin(turn) * scale], 1)

    move = np.zeros((MAP, MAP))
    for row, (h, w, ok) in enumerate(cell):
        if ok:
            move[row, h * WIDE + w] = 1.0
    in_high, in_low = split_matrix(forward(plain, -1.0))
    spread = np.concatenate([move, 0.0 * move], 1).astype(BF16)
    from_plain = np.concatenate([np.concatenate([in_high, in_low], 1), spread], 0)
    cell_high, cell_low = split_matrix(forward(cell, -1.0))
    from_cell = np.concatenate([cell_high, cell_low, cell_high], 1)
    high, low = split_matrix(backward(cell))
    to_cell = np.concatenate([high, high, low], 1)
    high, low = split_matrix(backward(plain))
    to_plain = np.concatenate([high, high, low, move.T.astype(BF16)], 1)
    high, low = split_matrix(forward(taps, 1.0) * RING)
    from_taps = np.concatenate([high, high, low], 1)
    high, low = split_matrix(backward(taps) * RING)
    to_taps = np.concatenate([high, high, low], 1)
    return from_plain, from_cell, to_cell, to_plain, from_taps, to_taps


def dot(left, right):
    return jnp.dot(left, right, preferred_element_type=F32)


def dot_rows(left, right):
    return lax.dot_general(left, right, (((0,), (0,)), ((), ())), preferred_element_type=F32)


def dot_cols(left, right):
    return lax.dot_general(left, right, (((1,), (1,)), ((), ())), preferred_element_type=F32)


def two_parts(value):
    high = value.astype(BF16)
    return high, (value - high.astype(F32)).astype(BF16)


def mean_of(value):
    return jnp.sum(value, axis=-1, keepdims=True) * (1.0 / C)


def fold(value):
    rows = value.shape[0]
    total = value[0:8]
    for at in range(8, rows, 8):
        total = total + value[at : at + 8]
    return total


def gelu_parts(value):
    below = 1.0 + jnp.abs(value) * (0.3275911 * 0.7071067811865476)
    t = pl.reciprocal(below, approx=True)
    t = t * (2.0 - below * t)
    bell = jnp.exp2(value * value * (-0.5 * 1.4426950408889634))
    tail = 0.5 * 1.061405429 * t - 0.5 * 1.453152027
    tail = tail * t + 0.5 * 1.421413741
    tail = tail * t - 0.5 * 0.284496736
    tail = tail * t + 0.5 * 0.254829592
    tail = tail * (t * bell)
    area = jnp.where(value >= 0.0, 1.0 - tail, tail)
    return value * area, area + value * (bell * 0.3989422804014327)


def alternate(steps, product, work, buffers):
    first, second = buffers
    product(0, first)

    def both(i, carry):
        product(2 * i + 1, second)
        carry = work(2 * i, first, carry)
        product(jnp.minimum(2 * i + 2, steps - 1), first)
        return work(2 * i + 1, second, carry)

    return functools.partial(lax.fori_loop, 0, steps // 2, both)


def put_split(store, rows, lanes, value):
    high, low = two_parts(value)
    at, count = rows
    store[pl.ds(at, count), lanes] = high
    store[pl.ds(SPEC + at, count), lanes] = low
    store[pl.ds(2 * SPEC + at, count), lanes] = high


def compute(own, first_image, keep_of, refs, grads, maps_out, image_out, small, s, at_point):
    (taps_in, kbias, gain1, shift1, bup, bdown, scale, gain2, shift2, bpatch, from_taps) = refs
    x, og, up, down, wpatch = s.x, s.og, s.up, s.down, s.wpatch
    from_cell, to_plain, to_taps = s.from_cell, s.to_plain, s.to_taps
    from_plain, to_cell = s.from_plain, s.to_cell
    pairs = own // 2
    groups = own * HALF

    def row(ref):
        return ref[...].reshape(1, -1)

    s.taps[...] = jnp.zeros((TAPS, C), F32)
    for i in range(7):
        s.taps[i * 8 : i * 8 + 7, :] = taps_in[i]
    high, low = two_parts(s.taps[...])
    s.khat[...] = dot(from_taps[...], jnp.concatenate([high, low, high], 0))

    at_point("og")
    images = s.x_in.shape[2]

    def take(a, carry):
        for b in range(HALF):
            v = s.og_in[a, b].astype(F32)
            for k in range(6):
                at = (8 * k + b) * images
                s.line[at : at + images, :] = v[:, k * 128 : k * 128 + 128]
        for n in range(own):
            at = pl.multiple_of((n * HALF + a) * 8, 8)
            for k in range(6):
                v = s.line[pl.ds(8 * k * images + first_image + n, 8, stride=images), :]
                s.maps[pl.ds(at, 8), k * 128 : k * 128 + 128] = v
        return carry

    for k in range(6):
        s.line[(8 * k + HALF) * images : (8 * k + 8) * images, :] = jnp.zeros((images, 128), F32)
    lax.fori_loop(0, HALF, take, 0)
    og[...] = s.maps[...].astype(BF16)

    at_point("x")
    plane = WIDE * images

    def widen(h, carry):
        for w in range(SIDE):
            v = s.x_in[h, w].astype(F32)
            for k in range(3):
                s.line[k * plane + w * images : k * plane + w * images + images, :] = v[:, k * 128 : k * 128 + 128]
        for n in range(own):
            for k in range(3):
                v = s.line[pl.ds(k * plane + first_image + n, WIDE, stride=images), :]
                x[n, pl.ds(pl.multiple_of(h * WIDE, WIDE), WIDE), k * 128 : k * 128 + 128] = v.astype(BF16)
        return carry

    for k in range(3):
        s.line[k * plane + SIDE * images : k * plane + plane, :] = jnp.zeros(((WIDE - SIDE) * images, 128), F32)
    lax.fori_loop(0, SIDE, widen, 0, unroll=2)

    bias_row, g1, s1 = row(kbias), row(gain1), row(shift1)

    at_point("f")

    def first(pair, carry):
        both = jnp.concatenate([x[2 * pair], x[2 * pair + 1]], 1)
        s.spec[pair] = dot(from_plain[:SPEC, :], jnp.concatenate([both, both], 0))
        s.moved[pair] = dot(from_plain[SPEC:, :MAP], both)

        def product(t, carry):
            at = pl.multiple_of(t * 16, 16)
            kre, kim = s.khat[pl.ds(at, 16), :], s.khat[pl.ds(FREQ + at, 16), :]
            for half in range(2):
                lanes = slice(half * C, half * C + C)
                re, im = s.spec[pair, pl.ds(at, 16), lanes], s.spec[pair, pl.ds(FREQ + at, 16), lanes]
                put_split(s.wave, (at, 16), lanes, re * kre - im * kim)
                put_split(s.wave, (FREQ + at, 16), lanes, im * kre + re * kim)
            return carry

        lax.fori_loop(0, FREQ // 16, product, 0, unroll=2)
        s.conv[...] = dot(to_cell[...], s.wave[: 3 * SPEC, :])

        def norm(t, carry):
            for half in range(2):
                for k in range(2):
                    at = pl.multiple_of(t * 32 + k * 16, 16)
                    v = s.conv[pl.ds(at, 16), half * C : half * C + C] + bias_row
                    v = v - mean_of(v)
                    r = lax.rsqrt(mean_of(v * v) + 1e-06)
                    n = v * r
                    to = pl.multiple_of((2 * pair + half) * MAP + at, 16)
                    s.n1[pl.ds(to, 16), :] = n
                    s.r1[pl.ds(to, 16), :] = r
                    s.normed[pl.ds(to, 16), :] = (n * g1 + s1).astype(BF16)
            return carry

        lax.fori_loop(0, MAP // 32, norm, 0, unroll=True)
        return carry

    lax.fori_loop(0, pairs, first, 0)

    wide = FF // 2
    block = 2 * MAP

    some = MAP // 2
    blocks = own * MAP // some

    def rows_of(k):
        return pl.ds(pl.multiple_of(k * some, 16), some)

    def expand(part):
        lanes = slice(part * wide, part * wide + wide)
        bias = row(bup)[:, lanes]

        def product(k, target):
            target[...] = dot(s.normed[rows_of(k), :], up[:, lanes])

        def curve(k, source, carry):
            for at in range(0, some, 16):
                to = pl.multiple_of(k * some + at, 16)
                for lane in range(0, wide, 256):
                    v = source[at : at + 16, lane : lane + 256] + bias[:, lane : lane + 256]
                    value, slope = gelu_parts(v)
                    s.act[part, pl.ds(to, 16), lane : lane + 256] = value.astype(BF16)
                    s.slope[part, pl.ds(to, 16), lane : lane + 256] = slope
            return carry

        alternate(blocks, product, curve, (s.hidden, s.hidden_too))(0)

    at_point("up")
    for part in range(2):
        expand(part)
    at_point("down")

    def reduce(pair, carry):
        rows = pl.ds(pl.multiple_of(pair * block, block), block)
        s.branch[rows, :] = (
            dot(s.act[0, rows, :], down[:wide, :]) + dot(s.act[1, rows, :], down[wide:, :]) + row(bdown)
        )
        return carry

    lax.fori_loop(0, pairs, reduce, 0)

    ls, g2, s2 = row(scale), row(gain2), row(shift2)

    def join(t, carry):
        for i in range(2):
            pieces = []
            for k in range(2):
                group = 4 * t + 2 * i + k
                factor = keep_of(group // HALF)
                at = pl.multiple_of(group * 32, 32)
                inside = pl.multiple_of((group % HALF) * 32, 32)
                image = group // HALF
                lane = pl.ds(pl.multiple_of((image % 2) * C, C), C)
                v = s.moved[image // 2, pl.ds(inside, 32), lane]
                v = v + factor * ls * s.branch[pl.ds(at, 32), :]
                v = v.astype(BF16).astype(F32)
                v = v - mean_of(v)
                r = lax.rsqrt(mean_of(v * v) + 1e-06)
                n = v * r
                s.n2[pl.ds(at, 32), :] = n
                s.r2[pl.ds(at, 32), :] = r
                pieces.append(n * g2 + s2)
            to = pl.multiple_of(t * 32 + i * 16, 16)
            for ij in range(4):
                both = jnp.concatenate([piece[ij * 8 : ij * 8 + 8] for piece in pieces], 0)
                s.patches[pl.ds(to, 16), ij * C : ij * C + C] = both.astype(BF16)
        return carry

    lax.fori_loop(0, groups // 4, join, 0)

    for ij in range(4):
        g = dot_rows(s.patches[:, ij * C : ij * C + C], og[...])
        grads[0, ij * C : ij * C + C, :] = g[:, :C].astype(BF16)
        grads[1, ij * C : ij * C + C, :] = g[:, C:].astype(BF16)
        if ij == 1:
            at_point("p0")
    at_point("p1")

    s.maps[...] = dot(s.patches[...], wpatch[...]) + row(bpatch)
    count = maps_out.shape[0]
    part = OUT // count

    def share(t, carry):
        at = pl.multiple_of(t * 16, 16)
        v = s.maps[pl.ds(at, 16), :]
        for q in range(count):
            turned = v if q == 0 else pltpu.roll(v, OUT - q * part, 1)
            maps_out[q, pl.ds(at, 16), :] = turned[:, :part].astype(BF16)
        return carry

    lax.fori_loop(0, own * CELLS // 16, share, 0, unroll=2)
    at_point("m")

    s.back[...] = dot_cols(og[...], wpatch[...])
    at_point("b")

    zero = jnp.zeros((8, C), F32)

    def unjoin(t, carry):
        for k in range(2):
            sum_gain, sum_shift, sum_scale, sum_bias = carry
            group = 2 * t + k
            factor = keep_of(group // HALF)
            from_row = pl.multiple_of(group * 8, 8)
            at = pl.multiple_of(group * 32, 32)
            m = s.back[pl.ds(from_row, 8), :]
            m = jnp.concatenate([m[:, ij * C : ij * C + C] for ij in range(4)], 0)
            n = s.n2[pl.ds(at, 32), :]
            sum_gain = sum_gain + fold(m * n)
            sum_shift = sum_shift + fold(m)
            e = m * g2
            back = s.r2[pl.ds(at, 32), :] * (e - mean_of(e) - n * mean_of(e * n))
            low = back.astype(BF16)
            back = low.astype(F32)
            image = group // HALF
            inside = pl.multiple_of((group % HALF) * 32, 32)
            s.rgrad[image, pl.ds(inside, 32), :] = low
            sum_scale = sum_scale + fold(back * s.branch[pl.ds(at, 32), :]) * factor
            bg = back * (factor * ls)
            s.bgrad[pl.ds(at, 32), :] = bg.astype(BF16)
            sum_bias = sum_bias + fold(bg)
            carry = sum_gain, sum_shift, sum_scale, sum_bias
        return carry

    sums = lax.fori_loop(0, groups // 4, unjoin, (zero,) * 4)
    at_point("j0")
    sum_gain, sum_shift, sum_scale, sum_bias = lax.fori_loop(groups // 4, groups // 2, unjoin, sums)
    for k, total in ((31, sum_bias), (39, sum_scale), (47, sum_gain), (55, sum_shift)):
        s.rows[k // 8 : k // 8 + 1, :] = jnp.sum(total, 0, keepdims=True)
    at_point("j")

    for part in range(2):
        g = dot_rows(s.act[part], s.bgrad[...])
        grads[2, part * wide : part * wide + wide, :] = g.astype(BF16)
        at_point("d0" if part == 0 else "d1")

    def slopes(part):
        def product(k, target):
            target[...] = dot_cols(s.bgrad[rows_of(k), :], down[part * wide : part * wide + wide, :])

        def times(k, source, carry):
            carry = list(carry)
            for at in range(0, some, 16):
                to = pl.multiple_of(k * some + at, 16)
                for i, lane in enumerate(range(0, wide, C)):
                    v = source[at : at + 16, lane : lane + C] * s.slope[part, pl.ds(to, 16), lane : lane + C]
                    s.act[part, pl.ds(to, 16), lane : lane + C] = v.astype(BF16)
                    carry[i] = carry[i] + fold(v)
            return tuple(carry)

        a, b = alternate(blocks, product, times, (s.hidden, s.hidden_too))((zero, zero))
        s.usum[part * 16 : part * 16 + 8, :] = a
        s.usum[part * 16 + 8 : part * 16 + 16, :] = b

    for part in range(2):
        slopes(part)
        at_point("s" + str(2 * part + 1))

    for part in range(2):
        g = dot_rows(s.normed[...], s.act[part])
        grads[3, 2 * part * C : 2 * part * C + C, :] = g[:, :C].astype(BF16)
        grads[3, 2 * part * C + C : 2 * part * C + 2 * C, :] = g[:, C:].astype(BF16)
        at_point("u0" if part == 0 else "u1")

    def narrow(pair, carry):
        rows = pl.ds(pl.multiple_of(pair * block, block), block)
        s.branch[rows, :] = dot_cols(s.act[0, rows, :], up[:, :wide]) + dot_cols(s.act[1, rows, :], up[:, wide:])
        return carry

    for pair in range(pairs):
        narrow(pair, 0)
        at_point("n0" if pair < pairs - 1 else "n")

    s.zhat[...] = jnp.zeros((SPEC, C), F32)

    def last(pair, carry):
        def unnorm(t, carry):
            for half in range(2):
                sum_gain, sum_shift, sum_bias = carry
                at = pl.multiple_of(t * 32, 32)
                to = pl.multiple_of((2 * pair + half) * MAP + at, 32)
                m = s.branch[pl.ds(to, 32), :]
                n = s.n1[pl.ds(to, 32), :]
                sum_gain = sum_gain + fold(m * n)
                sum_shift = sum_shift + fold(m)
                e = m * g1
                back = s.r1[pl.ds(to, 32), :] * (e - mean_of(e) - n * mean_of(e * n))
                sum_bias = sum_bias + fold(back)
                high, low = two_parts(back)
                lanes = slice(half * C, half * C + C)
                s.chigh[pl.ds(at, 32), lanes] = high
                s.clow[pl.ds(at, 32), lanes] = low
                s.wave[pl.ds(3 * SPEC + at, 32), lanes] = s.rgrad[2 * pair + half, pl.ds(at, 32), :]
                carry = sum_gain, sum_shift, sum_bias
            return carry

        carry = lax.fori_loop(0, MAP // 32, unnorm, carry, unroll=True)
        at_point("l" + str(3 * pair))
        high = s.chigh[...]
        s.ghat[...] = dot(from_cell[...], jnp.concatenate([high, high, s.clow[...]], 0))
        at_point("l" + str(3 * pair + 1))

        def product(t, carry):
            at = pl.multiple_of(t * 16, 16)
            kre, kim = s.khat[pl.ds(at, 16), :], s.khat[pl.ds(FREQ + at, 16), :]
            zre, zim = s.zhat[pl.ds(at, 16), :], s.zhat[pl.ds(FREQ + at, 16), :]
            for half in range(2):
                lanes = slice(half * C, half * C + C)
                re, im = s.ghat[pl.ds(at, 16), lanes], s.ghat[pl.ds(FREQ + at, 16), lanes]
                xre, xim = s.spec[pair, pl.ds(at, 16), lanes], s.spec[pair, pl.ds(FREQ + at, 16), lanes]
                zre = zre + re * xre + im * xim
                zim = zim + re * xim - im * xre
                put_split(s.wave, (at, 16), lanes, re * kre + im * kim)
                put_split(s.wave, (FREQ + at, 16), lanes, im * kre - re * kim)
            s.zhat[pl.ds(at, 16), :] = zre
            s.zhat[pl.ds(FREQ + at, 16), :] = zim
            return carry

        lax.fori_loop(0, FREQ // 16, product, 0, unroll=2)
        s.moved[pair] = dot(to_plain[...], s.wave[...])
        return carry

    carry = (zero,) * 3
    for pair in range(pairs):
        carry = last(pair, carry)
        at_point("l" + str(3 * pair + 2))
    sum_gain, sum_shift, sum_bias = carry

    def pack(t, carry):
        at = pl.multiple_of(t * 16, 16)
        lanes = lax.broadcasted_iota(jnp.int32, (16, C), 1)
        values = [s.moved[n // 2, pl.ds(at, 16), (n % 2) * C : (n % 2) * C + C] for n in range(own)]
        size = C // count
        for q in range(count):
            total = None
            for n in range(own):
                turn = ((n - q) * size) % C
                v = values[n] if turn == 0 else pltpu.roll(values[n], turn, 1)
                total = v if total is None else jnp.where(lanes >= n * size, v, total)
            image_out[q, pl.ds(at, 16), :] = total.astype(BF16)
        return carry

    lax.fori_loop(0, MAP // 16, pack, 0)
    at_point("i")

    zhigh, zlow = two_parts(s.zhat[...])
    small[0:TAPS, :] = dot(to_taps[...], jnp.concatenate([zhigh, zlow, zhigh], 0))
    small[7:8, :] = jnp.sum(sum_bias, 0, keepdims=True)
    small[15:16, :] = jnp.sum(sum_gain, 0, keepdims=True)
    small[23:24, :] = jnp.sum(sum_shift, 0, keepdims=True)
    for k in range(3, 7):
        small[8 * k + 7 : 8 * k + 8, :] = s.rows[k : k + 1, :]
    for k in range(4):
        small[56 + k : 57 + k, :] = jnp.sum(s.usum[k * 8 : k * 8 + 8, :], 0, keepdims=True)
    ones = fold(og[...].astype(F32))
    ones = jnp.sum(ones, 0, keepdims=True)
    small[60:61, :] = ones[:, :C]
    small[61:62, :] = ones[:, C:]
    small[62:64, :] = jnp.zeros((2, C), F32)
    at_point("t")


def scratch(own, ways, groups):
    count = own * ways
    steps = sum(groups_of(groups, ways), [])
    sum_rows, sum_copies = landing(2 * C, 16, steps)
    small_rows, small_copies = landing(SMALL, SMALL // 2, steps)
    rows = own * MAP
    pairs = own // 2
    return dict(
        x_in=pltpu.VMEM((SIDE, SIDE, count, C), BF16),
        line=pltpu.VMEM((3 * WIDE * count, 128), F32),
        x=pltpu.VMEM((own, MAP, C), BF16),
        og_in=pltpu.VMEM((HALF, HALF, count, OUT), BF16),
        og=pltpu.VMEM((own * CELLS, OUT), BF16),
        up=pltpu.VMEM((C, FF), BF16),
        down=pltpu.VMEM((FF, C), BF16),
        wpatch=pltpu.VMEM((4 * C, OUT), BF16),
        from_cell=pltpu.VMEM((SPEC, 3 * MAP), BF16),
        to_plain=pltpu.VMEM((MAP, 3 * SPEC + MAP), BF16),
        to_taps=pltpu.VMEM((TAPS, 3 * SPEC), BF16),
        in_sem=pltpu.SemaphoreType.DMA((10,)),
        from_plain=pltpu.VMEM((SPEC + MAP, 2 * MAP), BF16),
        to_cell=pltpu.VMEM((MAP, 3 * SPEC), BF16),
        taps=pltpu.VMEM((TAPS, C), F32),
        khat=pltpu.VMEM((SPEC, C), F32),
        spec=pltpu.VMEM((pairs, SPEC, 2 * C), F32),
        moved=pltpu.VMEM((pairs, MAP, 2 * C), F32),
        wave=pltpu.VMEM((3 * SPEC + MAP, 2 * C), BF16),
        conv=pltpu.VMEM((MAP, 2 * C), F32),
        n1=pltpu.VMEM((rows, C), F32),
        r1=pltpu.VMEM((rows, 1), F32),
        normed=pltpu.VMEM((rows, C), BF16),
        hidden=pltpu.VMEM((MAP // 2, FF // 2), F32),
        hidden_too=pltpu.VMEM((MAP // 2, FF // 2), F32),
        act=pltpu.VMEM((2, rows, FF // 2), BF16),
        slope=pltpu.VMEM((2, rows, FF // 2), F32),
        branch=pltpu.VMEM((rows, C), F32),
        n2=pltpu.VMEM((rows, C), F32),
        r2=pltpu.VMEM((rows, 1), F32),
        patches=pltpu.VMEM((own * CELLS, 4 * C), BF16),
        maps=pltpu.VMEM((own * CELLS, OUT), F32),
        back=pltpu.VMEM((own * CELLS, 4 * C), F32),
        rgrad=pltpu.VMEM((own, MAP, C), BF16),
        bgrad=pltpu.VMEM((rows, C), BF16),
        usum=pltpu.VMEM((32, C), F32),
        rows=pltpu.VMEM((8, C), F32),
        zhat=pltpu.VMEM((SPEC, C), F32),
        ghat=pltpu.VMEM((SPEC, 2 * C), F32),
        chigh=pltpu.VMEM((MAP, 2 * C), BF16),
        clow=pltpu.VMEM((MAP, 2 * C), BF16),
        grads=pltpu.VMEM((4, 4 * C, C), BF16),
        land=pltpu.VMEM((8, sum_rows, C), BF16),
        small=pltpu.VMEM((SMALL, C), F32),
        small_land=pltpu.VMEM((small_rows, C), F32),
        maps_out=pltpu.VMEM((ways, own * CELLS, OUT // ways), BF16),
        maps_in=pltpu.VMEM((ways, own * CELLS, OUT // ways), BF16),
        maps_held=pltpu.VMEM((ways, own * CELLS, -(-OUT // ways // 128) * 128), F32),
        image_out=pltpu.VMEM((ways, MAP, C), BF16),
        sum_send=pltpu.SemaphoreType.DMA((8, sum_copies)),
        sum_recv=pltpu.SemaphoreType.DMA((8, sum_copies)),
        small_send=pltpu.SemaphoreType.DMA((small_copies,)),
        small_recv=pltpu.SemaphoreType.DMA((small_copies,)),
        maps_send=pltpu.SemaphoreType.DMA((ways,)),
        maps_recv=pltpu.SemaphoreType.DMA((ways,)),
        image_send=pltpu.SemaphoreType.DMA((ways,)),
        image_recv=pltpu.SemaphoreType.DMA((ways,)),
    )


def landing(rows, least, steps):
    total, copies = 0, 0
    for at, bits in enumerate(steps):
        ways = 2**bits
        halving = rows % (ways * least) == 0 and at < len(steps) - 1
        rows = rows // ways if halving else rows
        total += (ways - 1) * rows
        copies += 2 * (ways - 1)
    return total, copies


class Sum:
    def __init__(self, work, land, total, rows, least, steps, sems):
        self.work, self.land, self.total = work, land, total
        self.steps, self.sems, self.least = steps, sems, least
        self.at, self.rows, self.start, self.used = 0, rows, 0, 0
        self.copies, self.path, self.slots, self.came = [], [], [], []
        self.count, self.halving, self.gathering = 0, True, False

    def send(self, source, target, axis, partner):
        copy = pltpu.make_async_remote_copy(
            src_ref=source,
            dst_ref=target,
            send_sem=self.sems[0].at[self.count],
            recv_sem=self.sems[1].at[self.count],
            device_id={axis: partner},
            device_id_type=pl.DeviceIdType.MESH,
        )
        copy.start()
        self.count += 1
        self.copies.append(copy)
        self.came.append(copy)

    def add(self, target, start, slots, rows):
        step = self.least
        while step < 64 and rows % (2 * step) == 0:
            step *= 2

        def one(t, carry):
            to = pl.ds(pl.multiple_of(start + t * step, self.least), step)
            total = self.work[to, :]
            for slot in slots:
                total = total + self.land[pl.ds(pl.multiple_of(slot + t * step, self.least), step), :]
            target[to, :] = total
            return carry

        lax.fori_loop(0, rows // step, one, 0)

    def reduce(self):
        start, rows, slots = self.start, self.rows, self.slots
        if self.came:
            for copy in self.came:
                copy.wait_recv()
            self.at += 1
            if self.at == len(self.steps):
                self.add(self.total, start, slots, rows)
                self.gather()
                return
            if not self.halving:
                for copy in self.came:
                    copy.wait_send()
                self.copies = self.copies[: len(self.copies) - len(self.came)]
        axis, index, bits = self.steps[self.at]
        ways = 2 ** len(bits)
        self.halving = rows % (ways * self.least) == 0 and self.at < len(self.steps) - 1
        count = rows // ways if self.halving else rows
        if slots and not self.halving:
            self.add(self.work, start, slots, rows)
        self.slots, self.came = [], []
        for mask in range(1, ways):
            partner, block = index, 0
            for k, (bit, delta) in enumerate(bits):
                away = mask >> k & 1
                partner = partner + away * delta
                block = block + (1 - bit if away else bit) * 2**k
            give = count * block if self.halving else 0
            if slots and self.halving:
                self.add(self.work, start + give, [slot + give for slot in slots], count)
            source = self.work.at[pl.ds(pl.multiple_of(start + give, self.least), count), :]
            self.send(source, self.land.at[pl.ds(self.used, count), :], axis, partner)
            self.slots.append(self.used)
            self.used += count
        keep = 0
        if self.halving:
            keep = count * sum(bit * 2**k for k, (bit, _) in enumerate(bits))
            self.path.append((axis, index, bits, start, rows))
            if slots:
                self.add(self.work, start + keep, [slot + keep for slot in slots], count)
        self.start, self.rows = start + keep, count

    def gather(self):
        self.gathering, self.came = True, []
        if self.path:
            axis, index, bits, start, rows = self.path.pop()
            here = self.total.at[pl.ds(pl.multiple_of(self.start, self.least), self.rows), :]
            for mask in range(1, 2 ** len(bits)):
                partner = index
                for k, (_, delta) in enumerate(bits):
                    partner = partner + (mask >> k & 1) * delta
                self.send(here, here, axis, partner)
            self.start, self.rows = start, rows

    def go(self):
        if not self.gathering:
            self.reduce()
        elif self.came:
            for copy in self.came:
                copy.wait_recv()
            self.gather()

    def running(self):
        return not self.gathering or bool(self.came)

    def finish(self):
        for copy in self.copies:
            copy.wait_send()


PARTS = ((0, 0), (1, 0), (0, 768), (1, 768), (2, 0), (2, 768), (3, 0), (3, 768))
IMAGE, MAPS = 100, 101
SCHEDULE = {
    "p0": (0,),
    "p1": (3,),
    "b": (0,),
    "j0": (2, MAPS, 1),
    "j": (3,),
    "d1": (5, 4, 2, 1),
    "s1": (0,),
    "u0": (6, 5, 3, 0),
    "u1": (4,),
    "n": (2, 1, 7, 3, 0, 6),
    "l2": (5, 7),
    "l3": (3, 0, 1),
    "l4": (2,),
    "l5": (6, 5, 3),
    "t": (8, 1, 4, 6),
    "end": (7, 8, 2, 0, 1, 5, 4, 3, 6, 7, 2, 8, 5, IMAGE, 4, 1, 3, 0, 6, 7, 1, 8, 4, 2, 5, 7, 6, 2, 4, 8, 7, 4, 8, 6, 5, 7),
}


def groups_of(groups, ways):
    left = groups.bit_length() - 1
    near = [1] if left else []
    left -= len(near)
    while left:
        near.append(min(2, left))
        left -= near[-1]
    return near, [1] * (ways.bit_length() - 1)


def routes(groups, ways):
    def steps(axis, sizes):
        index, stride, found = lax.axis_index(axis), 1, []
        for size in sizes:
            bits = []
            for _ in range(size):
                bit = lax.rem(lax.div(index, stride), 2)
                bits.append((bit, stride * (1 - 2 * bit)))
                stride *= 2
            found.append((axis, index, bits))
        return found

    near, far = groups_of(groups, ways)
    return steps("dp", near), steps("pipe", far)


def unpack_maps(own, ways, low, held, tall, cells):
    part, count = low.shape[2], own * ways

    def hold(t, carry):
        rows = pl.ds(pl.multiple_of(t * 16, 16), 16)
        for q in range(ways):
            held[q, rows, :part] = low[q, rows, :].astype(F32)
        return carry

    def unmap(a, carry):
        for lane in range(0, part, 128):
            for q in range(ways):
                for n in range(own):
                    v = held[q, pl.ds(pl.multiple_of((n * HALF + a) * 8, 8), 8), lane : lane + 128]
                    tall[pl.ds(lane // 128 * 8 * count + q * own + n, 8, stride=count), :] = v
            for b in range(HALF):
                at = lane // 128 * 8 * count + b * count
                v = tall[at : at + count, : min(128, part - lane)]
                cells[a, b, :, lane : min(lane + 128, part)] = v.astype(BF16)
        return carry

    lax.fori_loop(0, own * CELLS // 16, hold, 0)
    lax.fori_loop(0, HALF, unmap, 0)


def exchange(ways, source, land, sems):
    p = lax.axis_index("pipe")
    copies = []
    for j in range(1, ways):
        q = lax.rem(p + j, ways)
        copy = pltpu.make_async_remote_copy(
            src_ref=source.at[q],
            dst_ref=land.at[p],
            send_sem=sems[0].at[j - 1],
            recv_sem=sems[1].at[j - 1],
            device_id={"pipe": q},
            device_id_type=pl.DeviceIdType.MESH,
        )
        copy.start()
        copies.append(copy)
    return copies


def whole_kernel(own, ways, groups, *refs):
    keep = refs[0]
    ins = refs[1:12]
    images, out_grad, up, down, wpatch, from_cell, to_plain, to_taps, from_plain, to_cell = refs[12:22]
    total, maps_all, image_in, small_total = refs[22:26]
    s = SimpleNamespace(**dict(zip(scratch(own, ways, groups), refs[26:])))
    p = lax.axis_index("pipe")
    start = p * own
    fetched = {}
    for k, (name, source, target) in enumerate(
        (
            ("g", out_grad, s.og_in),
            ("x", images, s.x_in),
            ("f", from_plain, s.from_plain),
            ("e", to_cell, s.to_cell),
            ("u", up, s.up),
            ("d", down, s.down),
            ("w", wpatch, s.wpatch),
            ("c", from_cell, s.from_cell),
            ("p", to_plain, s.to_plain),
            ("t", to_taps, s.to_taps),
        )
    ):
        fetched[name] = pltpu.make_async_copy(source, target, s.in_sem.at[k])
        fetched[name].start()

    def keep_of(image):
        return keep[start + image].astype(F32) / 0.9

    near, far = routes(groups, ways)
    barrier = pltpu.get_barrier_semaphore()
    met = [("pipe", lax.rem(p + j, ways)) for j in range(1, ways)]
    for axis, index, bits in near:
        for mask in range(1, 2 ** len(bits)):
            met.append((axis, index + sum((mask >> k & 1) * delta for k, (_, delta) in enumerate(bits))))
    for axis, partner in met:
        pl.semaphore_signal(barrier, inc=1, device_id={axis: partner}, device_id_type=pl.DeviceIdType.MESH)

    steps = near + far

    def part_sum(i, k, first):
        rows = pl.ds(first, 2 * C)

        return Sum(
            s.grads.at[k, rows, :], s.land.at[i], total.at[k, rows, :], 2 * C, 16, steps,
            (s.sum_send.at[i], s.sum_recv.at[i]),
        )

    sums = [part_sum(i, k, first) for i, (k, first) in enumerate(PARTS)]
    tail = Sum(
        s.small, s.small_land, small_total, SMALL, SMALL // 2, steps, (s.small_send, s.small_recv)
    )
    chains = sums + [tail]
    kept = {}
    needs = {"og": "g", "x": "x", "f": "fe", "up": "u", "down": "d", "p0": "w", "n": "cpt"}

    def at_point(name):
        for needed in needs.get(name, ""):
            fetched[needed].wait()
        if name == "p0":
            pl.semaphore_wait(barrier, len(met))
        if name == "l4":
            for copy in kept[MAPS]:
                copy.wait_recv()
            unpack_maps(own, ways, s.maps_in, s.maps_held, s.line, maps_all)
        for k in SCHEDULE.get(name, ()):
            if k == MAPS:
                kept[k] = exchange(ways, s.maps_out, s.maps_in, (s.maps_send, s.maps_recv))
                s.maps_in[p] = s.maps_out[p]
            elif k == IMAGE:
                kept[k] = exchange(ways, s.image_out, image_in, (s.image_send, s.image_recv))
                image_in[p] = s.image_out[p]
            else:
                chains[k].go()

    compute(own, start, keep_of, ins, s.grads, s.maps_out, s.image_out, s.small, s, at_point)
    at_point("end")
    while any(chain.running() for chain in chains):
        for chain in chains:
            if chain.running():
                chain.go()
    exchanged = kept[MAPS] + kept[IMAGE]
    for copy in kept[IMAGE]:
        copy.wait_recv()
    for copy in exchanged:
        copy.wait_send()
    for chain in chains:
        chain.finish()


def whole_call(own, ways, groups, args):
    vmem = pl.BlockSpec(memory_space=pltpu.VMEM)
    away = pl.BlockSpec(memory_space=pl.ANY)
    return pl.pallas_call(
        functools.partial(whole_kernel, own, ways, groups),
        out_shape=(
            pltpu.VMEM((4, 4 * C, C), BF16),
            pltpu.VMEM((HALF, HALF, own * ways, OUT // ways), BF16),
            pltpu.VMEM((ways, MAP, C), BF16),
            jax.ShapeDtypeStruct((SMALL, C), F32),
        ),
        in_specs=[pl.BlockSpec(memory_space=pltpu.SMEM)] + [vmem] * 11 + [away] * 10,
        out_specs=[vmem] * 4,
        scratch_shapes=list(scratch(own, ways, groups).values()),
        compiler_params=pltpu.CompilerParams(
            collective_id=0, has_side_effects=True, vmem_limit_bytes=57 * 2**20
        ),
    )(*args)


def finish_kernel(own, ways, grads, maps, image, small, *refs):
    (merged, image_grad, taps, kbias, gain1, shift1, up_grad, up_bias, down_grad, down_bias, scale, gain2,
     shift2, patch_grad, patch_bias, patches, downs, ups, images, tall, sems) = refs
    size, count = C // ways, own * ways

    def block(c):
        return pl.ds(c * C, C)

    sent = []

    def send(source, target):
        copy = pltpu.make_async_copy(source, target, sems.at[len(sent)])
        copy.start()
        sent.append(copy)

    def widen(k, c, target, row, lane):
        def step(t, carry):
            at = t * 32
            target[pl.ds(pl.multiple_of(row + at, 32), 32), lane : lane + C] = grads[
                k, pl.ds(pl.multiple_of(c * C + at, 32), 32), :
            ].astype(F32)
            return carry

        lax.fori_loop(0, C // 32, step, 0, unroll=4)

    def patch(c):
        widen(0, c, patches, c * C, 0)
        widen(1, c, patches, c * C, C)
        send(patches.at[block(c), :], patch_grad.at[block(c), :])

    send(maps, merged)

    def unpack(h, carry):
        for q in range(ways):
            v = image[q, pl.ds(pl.multiple_of(h * WIDE, WIDE), WIDE), :].astype(F32)
            for n in range(own):
                first = n * size // 128 * 128
                turn = v[:, first : min(first + 256, C)]
                if n * size > first:
                    turn = pltpu.roll(turn, turn.shape[1] - (n * size - first), 1)
                tall[pl.ds(q * own + n, WIDE, stride=count), :] = turn[:, :128]
        for w in range(SIDE):
            images[h, w] = tall[w * count : w * count + count, :size]
        return carry

    for c in range(2):
        patch(c)
        rows = pl.ds(c * HALF, HALF)
        lax.fori_loop(c * HALF, c * HALF + HALF, unpack, 0)
        send(images.at[rows], image_grad.at[rows])
    patch(2)
    patch(3)
    for c in range(4):
        widen(2, c, downs, c * C, 0)
        if c % 2:
            rows = pl.ds((c - 1) * C, 2 * C)
            send(downs.at[rows, :], down_grad.at[rows, :])
    for c in range(4):
        widen(3, c, ups, 0, c * C)
        if c % 2:
            lanes = pl.ds((c - 1) * C, 2 * C)
            send(ups.at[:, lanes], up_grad.at[:, lanes])
    for i in range(7):
        taps[i] = small[i * 8 : i * 8 + 7, :]
    for i, out in enumerate((kbias, gain1, shift1, down_bias, scale, gain2, shift2)):
        out[...] = small[i * 8 + 7 : i * 8 + 8, :].reshape(C)
    for k in range(4):
        up_bias[k * C : k * C + C] = small[TAPS + k : TAPS + k + 1, :].reshape(C)
    for k in range(2):
        patch_bias[k * C : k * C + C] = small[TAPS + 4 + k : TAPS + 5 + k, :].reshape(C)
    for copy in sent:
        copy.wait()


def finish_call(own, ways, grads, maps, image, small):
    count = ways * own
    size, part = C // ways, OUT // ways
    vector = jax.ShapeDtypeStruct((C,), F32)
    shapes = (
        jax.ShapeDtypeStruct((HALF, HALF, count, part), BF16),
        jax.ShapeDtypeStruct((SIDE, SIDE, count, size), F32),
        jax.ShapeDtypeStruct((7, 7, C), F32),
        vector,
        vector,
        vector,
        jax.ShapeDtypeStruct((C, FF), F32),
        jax.ShapeDtypeStruct((FF,), F32),
        jax.ShapeDtypeStruct((FF, C), F32),
        vector,
        vector,
        vector,
        vector,
        jax.ShapeDtypeStruct((4 * C, OUT), F32),
        jax.ShapeDtypeStruct((OUT,), F32),
    )
    away = pl.BlockSpec(memory_space=pl.ANY)
    near = pl.BlockSpec(memory_space=pltpu.VMEM)
    outs = pl.pallas_call(
        functools.partial(finish_kernel, own, ways),
        out_shape=shapes,
        in_specs=[near] * 4,
        out_specs=[away if k in (0, 1, 6, 8, 13) else near for k in range(15)],
        scratch_shapes=[
            pltpu.VMEM((4 * C, OUT), F32),
            pltpu.VMEM((FF, C), F32),
            pltpu.VMEM((C, FF), F32),
            pltpu.VMEM((SIDE, SIDE, count, size), F32),
            pltpu.VMEM((WIDE * count, 128), F32),
            pltpu.SemaphoreType.DMA((32,)),
        ],
        compiler_params=pltpu.CompilerParams(vmem_limit_bytes=50 * 2**20),
    )(*[pltpu.with_memory_space_constraint(v, pltpu.VMEM) for v in (grads, maps, image)], small)
    return (outs[0].transpose(2, 0, 1, 3), outs[1].transpose(2, 0, 1, 3)) + tuple(outs[2:])


def shards(
    images, depth_kernel, depth_bias, norm_gain, norm_shift, up_weight, up_bias, down_weight, down_bias,
    layer_scale, merge_gain, merge_shift, patch_weight, patch_bias, keep_mask, out_grad,
):
    ways = lax.axis_size("pipe")
    own = images.shape[0] // ways
    from_plain, from_cell, to_cell, to_plain, from_taps, to_taps = [jnp.asarray(m) for m in transforms()]
    packed = whole_call(
        own, ways, lax.axis_size("dp"),
        (keep_mask, depth_kernel, depth_bias, norm_gain, norm_shift, up_bias, down_bias, layer_scale,
         merge_gain, merge_shift, patch_bias, from_taps,
         images.transpose(1, 2, 0, 3), out_grad.transpose(1, 2, 0, 3), up_weight, down_weight, patch_weight,
         from_cell, to_plain, to_taps, from_plain, to_cell),
    )
    return finish_call(own, ways, *packed)


def solution(mesh):
    whole = P()
    split = P("dp")
    placed = (split,) + (whole,) * 13 + (split, split)
    owned = P("dp", None, None, "pipe")
    return jax.shard_map(
        shards, mesh=mesh, in_specs=placed, out_specs=(owned, owned) + (whole,) * 13, check_vma=False
    )
```

```python
import functools
from types import SimpleNamespace

import jax
import jax.numpy as jnp
import numpy as np
from jax import lax
from jax.experimental import pallas as pl
from jax.experimental.pallas import tpu as pltpu
from jax.sharding import PartitionSpec as P

C = 384
FF = 1536
OUT = 768
SIDE = 14
WIDE = 16
HALF = 7
RING = SIDE + 3
FREQ = 160
SPEC = 2 * FREQ
MAP = SIDE * WIDE
CELLS = HALF * 8
TAPS = 56
SMALL = 64
F32 = jnp.float32
BF16 = jnp.bfloat16


def split_matrix(matrix):
    high = matrix.astype(BF16)
    low = (matrix - high.astype(np.float64)).astype(BF16)
    return high, low


def transforms():
    pairs = [(0, 0)] + [(u, 0) for u in range(1, 9)] + [(u, v) for v in range(1, 9) for u in range(RING)]
    freq = np.zeros((FREQ, 2))
    freq[: len(pairs)] = np.array(pairs)
    live = (np.arange(FREQ) < len(pairs)).astype(np.float64)
    weight = np.where(np.arange(FREQ) == 0, 1.0, 2.0) * live
    plain = np.array([(h, w, w < SIDE) for h in range(SIDE) for w in range(WIDE)])
    cell = np.array(
        [(h, 2 * b + j, b < HALF) for h in range(SIDE) for j in range(2) for b in range(8)]
    )
    taps = np.array([(i - 3, j - 3, j < 7) for i in range(7) for j in range(8)])

    def angles(places):
        return 2 * np.pi / RING * (freq @ places[:, :2].T)

    def forward(places, sign):
        turn = angles(places)
        scale = places[:, 2][None, :] * live[:, None] / RING
        return np.concatenate([np.cos(turn) * scale, sign * np.sin(turn) * scale], 0)

    def backward(places):
        turn = angles(places).T
        scale = places[:, 2][:, None] * weight[None, :] / RING
        return np.concatenate([np.cos(turn) * scale, -np.sin(turn) * scale], 1)

    move = np.zeros((MAP, MAP))
    for row, (h, w, ok) in enumerate(cell):
        if ok:
            move[row, h * WIDE + w] = 1.0
    in_high, in_low = split_matrix(forward(plain, -1.0))
    spread = np.concatenate([move, 0.0 * move], 1).astype(BF16)
    from_plain = np.concatenate([np.concatenate([in_high, in_low], 1), spread], 0)
    cell_high, cell_low = split_matrix(forward(cell, -1.0))
    from_cell = np.concatenate([cell_high, cell_low, cell_high], 1)
    high, low = split_matrix(backward(cell))
    to_cell = np.concatenate([high, high, low], 1)
    high, low = split_matrix(backward(plain))
    to_plain = np.concatenate([high, high, low, move.T.astype(BF16)], 1)
    high, low = split_matrix(forward(taps, 1.0) * RING)
    from_taps = np.concatenate([high, high, low], 1)
    high, low = split_matrix(backward(taps) * RING)
    to_taps = np.concatenate([high, high, low], 1)
    return from_plain, from_cell, to_cell, to_plain, from_taps, to_taps


def dot(left, right):
    return jnp.dot(left, right, preferred_element_type=F32)


def dot_rows(left, right):
    return lax.dot_general(left, right, (((0,), (0,)), ((), ())), preferred_element_type=F32)


def dot_cols(left, right):
    return lax.dot_general(left, right, (((1,), (1,)), ((), ())), preferred_element_type=F32)


def two_parts(value):
    high = value.astype(BF16)
    return high, (value - high.astype(F32)).astype(BF16)


def mean_of(value):
    return jnp.sum(value, axis=-1, keepdims=True) * (1.0 / C)


def fold(value):
    rows = value.shape[0]
    total = value[0:8]
    for at in range(8, rows, 8):
        total = total + value[at : at + 8]
    return total


def gelu_parts(value):
    below = 1.0 + jnp.abs(value) * (0.3275911 * 0.7071067811865476)
    t = pl.reciprocal(below, approx=True)
    t = t * (2.0 - below * t)
    bell = jnp.exp2(value * value * (-0.5 * 1.4426950408889634))
    tail = 0.5 * 1.061405429 * t - 0.5 * 1.453152027
    tail = tail * t + 0.5 * 1.421413741
    tail = tail * t - 0.5 * 0.284496736
    tail = tail * t + 0.5 * 0.254829592
    tail = tail * (t * bell)
    area = jnp.where(value >= 0.0, 1.0 - tail, tail)
    return value * area, area + value * (bell * 0.3989422804014327)


def alternate(steps, product, work, buffers):
    first, second = buffers
    product(0, first)

    def both(i, carry):
        product(2 * i + 1, second)
        carry = work(2 * i, first, carry)
        product(jnp.minimum(2 * i + 2, steps - 1), first)
        return work(2 * i + 1, second, carry)

    return functools.partial(lax.fori_loop, 0, steps // 2, both)


def put_split(store, rows, lanes, value):
    high, low = two_parts(value)
    at, count = rows
    store[pl.ds(at, count), lanes] = high
    store[pl.ds(SPEC + at, count), lanes] = low
    store[pl.ds(2 * SPEC + at, count), lanes] = high


def compute(own, first_image, keep_of, refs, grads, maps_out, image_out, small, s, at_point):
    (taps_in, kbias, gain1, shift1, bup, bdown, scale, gain2, shift2, bpatch, from_taps) = refs
    x, og, up, down, wpatch = s.x, s.og, s.up, s.down, s.wpatch
    from_cell, to_plain, to_taps = s.from_cell, s.to_plain, s.to_taps
    from_plain, to_cell = s.from_plain, s.to_cell
    pairs = own // 2
    groups = own * HALF

    def row(ref):
        return ref[...].reshape(1, -1)

    s.taps[...] = jnp.zeros((TAPS, C), F32)
    for i in range(7):
        s.taps[i * 8 : i * 8 + 7, :] = taps_in[i]
    high, low = two_parts(s.taps[...])
    s.khat[...] = dot(from_taps[...], jnp.concatenate([high, low, high], 0))

    at_point("og")
    images = s.x_in.shape[2]

    def take(a, carry):
        for b in range(HALF):
            v = s.og_in[a, b].astype(F32)
            for k in range(6):
                at = (8 * k + b) * images
                s.line[at : at + images, :] = v[:, k * 128 : k * 128 + 128]
        for n in range(own):
            at = pl.multiple_of((n * HALF + a) * 8, 8)
            for k in range(6):
                v = s.line[pl.ds(8 * k * images + first_image + n, 8, stride=images), :]
                s.maps[pl.ds(at, 8), k * 128 : k * 128 + 128] = v
        return carry

    for k in range(6):
        s.line[(8 * k + HALF) * images : (8 * k + 8) * images, :] = jnp.zeros((images, 128), F32)
    lax.fori_loop(0, HALF, take, 0)
    og[...] = s.maps[...].astype(BF16)

    at_point("x")
    plane = WIDE * images

    def widen(h, carry):
        for w in range(SIDE):
            v = s.x_in[h, w].astype(F32)
            for k in range(3):
                s.line[k * plane + w * images : k * plane + w * images + images, :] = v[:, k * 128 : k * 128 + 128]
        for n in range(own):
            for k in range(3):
                v = s.line[pl.ds(k * plane + first_image + n, WIDE, stride=images), :]
                x[n, pl.ds(pl.multiple_of(h * WIDE, WIDE), WIDE), k * 128 : k * 128 + 128] = v.astype(BF16)
        return carry

    for k in range(3):
        s.line[k * plane + SIDE * images : k * plane + plane, :] = jnp.zeros(((WIDE - SIDE) * images, 128), F32)
    lax.fori_loop(0, SIDE, widen, 0, unroll=2)

    bias_row, g1, s1 = row(kbias), row(gain1), row(shift1)

    at_point("f")

    def first(pair, carry):
        both = jnp.concatenate([x[2 * pair], x[2 * pair + 1]], 1)
        s.spec[pair] = dot(from_plain[:SPEC, :], jnp.concatenate([both, both], 0))
        s.moved[pair] = dot(from_plain[SPEC:, :MAP], both)

        def product(t, carry):
            at = pl.multiple_of(t * 16, 16)
            kre, kim = s.khat[pl.ds(at, 16), :], s.khat[pl.ds(FREQ + at, 16), :]
            for half in range(2):
                lanes = slice(half * C, half * C + C)
                re, im = s.spec[pair, pl.ds(at, 16), lanes], s.spec[pair, pl.ds(FREQ + at, 16), lanes]
                put_split(s.wave, (at, 16), lanes, re * kre - im * kim)
                put_split(s.wave, (FREQ + at, 16), lanes, im * kre + re * kim)
            return carry

        lax.fori_loop(0, FREQ // 16, product, 0, unroll=2)
        s.conv[...] = dot(to_cell[...], s.wave[: 3 * SPEC, :])

        def norm(t, carry):
            for half in range(2):
                for k in range(2):
                    at = pl.multiple_of(t * 32 + k * 16, 16)
                    v = s.conv[pl.ds(at, 16), half * C : half * C + C] + bias_row
                    v = v - mean_of(v)
                    r = lax.rsqrt(mean_of(v * v) + 1e-06)
                    n = v * r
                    to = pl.multiple_of((2 * pair + half) * MAP + at, 16)
                    s.n1[pl.ds(to, 16), :] = n
                    s.r1[pl.ds(to, 16), :] = r
                    s.normed[pl.ds(to, 16), :] = (n * g1 + s1).astype(BF16)
            return carry

        lax.fori_loop(0, MAP // 32, norm, 0, unroll=True)
        return carry

    lax.fori_loop(0, pairs, first, 0)

    wide = FF // 2
    block = 2 * MAP

    some = MAP // 2
    blocks = own * MAP // some

    def rows_of(k):
        return pl.ds(pl.multiple_of(k * some, 16), some)

    def expand(part):
        lanes = slice(part * wide, part * wide + wide)
        bias = row(bup)[:, lanes]

        def product(k, target):
            target[...] = dot(s.normed[rows_of(k), :], up[:, lanes])

        def curve(k, source, carry):
            for at in range(0, some, 16):
                to = pl.multiple_of(k * some + at, 16)
                for lane in range(0, wide, 256):
                    v = source[at : at + 16, lane : lane + 256] + bias[:, lane : lane + 256]
                    value, slope = gelu_parts(v)
                    s.act[part, pl.ds(to, 16), lane : lane + 256] = value.astype(BF16)
                    s.slope[part, pl.ds(to, 16), lane : lane + 256] = slope
            return carry

        alternate(blocks, product, curve, (s.hidden, s.hidden_too))(0)

    at_point("up")
    for part in range(2):
        expand(part)
    at_point("down")

    def reduce(pair, carry):
        rows = pl.ds(pl.multiple_of(pair * block, block), block)
        s.branch[rows, :] = (
            dot(s.act[0, rows, :], down[:wide, :]) + dot(s.act[1, rows, :], down[wide:, :]) + row(bdown)
        )
        return carry

    lax.fori_loop(0, pairs, reduce, 0)

    ls, g2, s2 = row(scale), row(gain2), row(shift2)

    def join(t, carry):
        for i in range(2):
            pieces = []
            for k in range(2):
                group = 4 * t + 2 * i + k
                factor = keep_of(group // HALF)
                at = pl.multiple_of(group * 32, 32)
                inside = pl.multiple_of((group % HALF) * 32, 32)
                image = group // HALF
                lane = pl.ds(pl.multiple_of((image % 2) * C, C), C)
                v = s.moved[image // 2, pl.ds(inside, 32), lane]
                v = v + factor * ls * s.branch[pl.ds(at, 32), :]
                v = v.astype(BF16).astype(F32)
                v = v - mean_of(v)
                r = lax.rsqrt(mean_of(v * v) + 1e-06)
                n = v * r
                s.n2[pl.ds(at, 32), :] = n
                s.r2[pl.ds(at, 32), :] = r
                pieces.append(n * g2 + s2)
            to = pl.multiple_of(t * 32 + i * 16, 16)
            for ij in range(4):
                both = jnp.concatenate([piece[ij * 8 : ij * 8 + 8] for piece in pieces], 0)
                s.patches[pl.ds(to, 16), ij * C : ij * C + C] = both.astype(BF16)
        return carry

    lax.fori_loop(0, groups // 4, join, 0)

    for ij in range(4):
        g = dot_rows(s.patches[:, ij * C : ij * C + C], og[...])
        grads[0, ij * C : ij * C + C, :] = g[:, :C].astype(BF16)
        grads[1, ij * C : ij * C + C, :] = g[:, C:].astype(BF16)
        if ij == 1:
            at_point("p0")
    at_point("p1")

    s.maps[...] = dot(s.patches[...], wpatch[...]) + row(bpatch)
    count = maps_out.shape[0]
    part = OUT // count

    def share(t, carry):
        at = pl.multiple_of(t * 16, 16)
        v = s.maps[pl.ds(at, 16), :]
        for q in range(count):
            turned = v if q == 0 else pltpu.roll(v, OUT - q * part, 1)
            maps_out[q, pl.ds(at, 16), :] = turned[:, :part].astype(BF16)
        return carry

    lax.fori_loop(0, own * CELLS // 16, share, 0, unroll=2)
    at_point("m")

    s.back[...] = dot_cols(og[...], wpatch[...])
    at_point("b")

    zero = jnp.zeros((8, C), F32)

    def unjoin(t, carry):
        for k in range(2):
            sum_gain, sum_shift, sum_scale, sum_bias = carry
            group = 2 * t + k
            factor = keep_of(group // HALF)
            from_row = pl.multiple_of(group * 8, 8)
            at = pl.multiple_of(group * 32, 32)
            m = s.back[pl.ds(from_row, 8), :]
            m = jnp.concatenate([m[:, ij * C : ij * C + C] for ij in range(4)], 0)
            n = s.n2[pl.ds(at, 32), :]
            sum_gain = sum_gain + fold(m * n)
            sum_shift = sum_shift + fold(m)
            e = m * g2
            back = s.r2[pl.ds(at, 32), :] * (e - mean_of(e) - n * mean_of(e * n))
            low = back.astype(BF16)
            back = low.astype(F32)
            image = group // HALF
            inside = pl.multiple_of((group % HALF) * 32, 32)
            s.rgrad[image, pl.ds(inside, 32), :] = low
            sum_scale = sum_scale + fold(back * s.branch[pl.ds(at, 32), :]) * factor
            bg = back * (factor * ls)
            s.bgrad[pl.ds(at, 32), :] = bg.astype(BF16)
            sum_bias = sum_bias + fold(bg)
            carry = sum_gain, sum_shift, sum_scale, sum_bias
        return carry

    sums = lax.fori_loop(0, groups // 4, unjoin, (zero,) * 4)
    at_point("j0")
    sum_gain, sum_shift, sum_scale, sum_bias = lax.fori_loop(groups // 4, groups // 2, unjoin, sums)
    for k, total in ((31, sum_bias), (39, sum_scale), (47, sum_gain), (55, sum_shift)):
        s.rows[k // 8 : k // 8 + 1, :] = jnp.sum(total, 0, keepdims=True)
    at_point("j")

    for part in range(2):
        g = dot_rows(s.act[part], s.bgrad[...])
        grads[2, part * wide : part * wide + wide, :] = g.astype(BF16)
        at_point("d0" if part == 0 else "d1")

    def slopes(part):
        def product(k, target):
            target[...] = dot_cols(s.bgrad[rows_of(k), :], down[part * wide : part * wide + wide, :])

        def times(k, source, carry):
            carry = list(carry)
            for at in range(0, some, 16):
                to = pl.multiple_of(k * some + at, 16)
                for i, lane in enumerate(range(0, wide, C)):
                    v = source[at : at + 16, lane : lane + C] * s.slope[part, pl.ds(to, 16), lane : lane + C]
                    s.act[part, pl.ds(to, 16), lane : lane + C] = v.astype(BF16)
                    carry[i] = carry[i] + fold(v)
            return tuple(carry)

        a, b = alternate(blocks, product, times, (s.hidden, s.hidden_too))((zero, zero))
        s.usum[part * 16 : part * 16 + 8, :] = a
        s.usum[part * 16 + 8 : part * 16 + 16, :] = b

    for part in range(2):
        slopes(part)
        at_point("s" + str(2 * part + 1))

    for part in range(2):
        g = dot_rows(s.normed[...], s.act[part])
        grads[3, 2 * part * C : 2 * part * C + C, :] = g[:, :C].astype(BF16)
        grads[3, 2 * part * C + C : 2 * part * C + 2 * C, :] = g[:, C:].astype(BF16)
        at_point("u0" if part == 0 else "u1")

    def narrow(pair, carry):
        rows = pl.ds(pl.multiple_of(pair * block, block), block)
        s.branch[rows, :] = dot_cols(s.act[0, rows, :], up[:, :wide]) + dot_cols(s.act[1, rows, :], up[:, wide:])
        return carry

    for pair in range(pairs):
        narrow(pair, 0)
        at_point("n0" if pair < pairs - 1 else "n")

    s.zhat[...] = jnp.zeros((SPEC, C), F32)

    def last(pair, carry):
        def unnorm(t, carry):
            for half in range(2):
                sum_gain, sum_shift, sum_bias = carry
                at = pl.multiple_of(t * 32, 32)
                to = pl.multiple_of((2 * pair + half) * MAP + at, 32)
                m = s.branch[pl.ds(to, 32), :]
                n = s.n1[pl.ds(to, 32), :]
                sum_gain = sum_gain + fold(m * n)
                sum_shift = sum_shift + fold(m)
                e = m * g1
                back = s.r1[pl.ds(to, 32), :] * (e - mean_of(e) - n * mean_of(e * n))
                sum_bias = sum_bias + fold(back)
                high, low = two_parts(back)
                lanes = slice(half * C, half * C + C)
                s.chigh[pl.ds(at, 32), lanes] = high
                s.clow[pl.ds(at, 32), lanes] = low
                s.wave[pl.ds(3 * SPEC + at, 32), lanes] = s.rgrad[2 * pair + half, pl.ds(at, 32), :]
                carry = sum_gain, sum_shift, sum_bias
            return carry

        carry = lax.fori_loop(0, MAP // 32, unnorm, carry, unroll=True)
        at_point("l" + str(3 * pair))
        high = s.chigh[...]
        s.ghat[...] = dot(from_cell[...], jnp.concatenate([high, high, s.clow[...]], 0))
        at_point("l" + str(3 * pair + 1))

        def product(t, carry):
            at = pl.multiple_of(t * 16, 16)
            kre, kim = s.khat[pl.ds(at, 16), :], s.khat[pl.ds(FREQ + at, 16), :]
            zre, zim = s.zhat[pl.ds(at, 16), :], s.zhat[pl.ds(FREQ + at, 16), :]
            for half in range(2):
                lanes = slice(half * C, half * C + C)
                re, im = s.ghat[pl.ds(at, 16), lanes], s.ghat[pl.ds(FREQ + at, 16), lanes]
                xre, xim = s.spec[pair, pl.ds(at, 16), lanes], s.spec[pair, pl.ds(FREQ + at, 16), lanes]
                zre = zre + re * xre + im * xim
                zim = zim + re * xim - im * xre
                put_split(s.wave, (at, 16), lanes, re * kre + im * kim)
                put_split(s.wave, (FREQ + at, 16), lanes, im * kre - re * kim)
            s.zhat[pl.ds(at, 16), :] = zre
            s.zhat[pl.ds(FREQ + at, 16), :] = zim
            return carry

        lax.fori_loop(0, FREQ // 16, product, 0, unroll=2)
        s.moved[pair] = dot(to_plain[...], s.wave[...])
        return carry

    carry = (zero,) * 3
    for pair in range(pairs):
        carry = last(pair, carry)
        at_point("l" + str(3 * pair + 2))
    sum_gain, sum_shift, sum_bias = carry

    def pack(t, carry):
        at = pl.multiple_of(t * 16, 16)
        lanes = lax.broadcasted_iota(jnp.int32, (16, C), 1)
        values = [s.moved[n // 2, pl.ds(at, 16), (n % 2) * C : (n % 2) * C + C] for n in range(own)]
        size = C // count
        for q in range(count):
            total = None
            for n in range(own):
                turn = ((n - q) * size) % C
                v = values[n] if turn == 0 else pltpu.roll(values[n], turn, 1)
                total = v if total is None else jnp.where(lanes >= n * size, v, total)
            image_out[q, pl.ds(at, 16), :] = total.astype(BF16)
        return carry

    lax.fori_loop(0, MAP // 16, pack, 0)
    at_point("i")

    zhigh, zlow = two_parts(s.zhat[...])
    small[0:TAPS, :] = dot(to_taps[...], jnp.concatenate([zhigh, zlow, zhigh], 0))
    small[7:8, :] = jnp.sum(sum_bias, 0, keepdims=True)
    small[15:16, :] = jnp.sum(sum_gain, 0, keepdims=True)
    small[23:24, :] = jnp.sum(sum_shift, 0, keepdims=True)
    for k in range(3, 7):
        small[8 * k + 7 : 8 * k + 8, :] = s.rows[k : k + 1, :]
    for k in range(4):
        small[56 + k : 57 + k, :] = jnp.sum(s.usum[k * 8 : k * 8 + 8, :], 0, keepdims=True)
    ones = fold(og[...].astype(F32))
    ones = jnp.sum(ones, 0, keepdims=True)
    small[60:61, :] = ones[:, :C]
    small[61:62, :] = ones[:, C:]
    small[62:64, :] = jnp.zeros((2, C), F32)
    at_point("t")


def scratch(own, ways, groups):
    count = own * ways
    steps = sum(groups_of(groups, ways), [])
    sum_rows, sum_copies = landing(2 * C, 16, steps)
    small_rows, small_copies = landing(SMALL, SMALL // 2, steps)
    rows = own * MAP
    pairs = own // 2
    return dict(
        x_in=pltpu.VMEM((SIDE, SIDE, count, C), BF16),
        line=pltpu.VMEM((3 * WIDE * count, 128), F32),
        x=pltpu.VMEM((own, MAP, C), BF16),
        og_in=pltpu.VMEM((HALF, HALF, count, OUT), BF16),
        og=pltpu.VMEM((own * CELLS, OUT), BF16),
        up=pltpu.VMEM((C, FF), BF16),
        down=pltpu.VMEM((FF, C), BF16),
        wpatch=pltpu.VMEM((4 * C, OUT), BF16),
        from_cell=pltpu.VMEM((SPEC, 3 * MAP), BF16),
        to_plain=pltpu.VMEM((MAP, 3 * SPEC + MAP), BF16),
        to_taps=pltpu.VMEM((TAPS, 3 * SPEC), BF16),
        in_sem=pltpu.SemaphoreType.DMA((10,)),
        from_plain=pltpu.VMEM((SPEC + MAP, 2 * MAP), BF16),
        to_cell=pltpu.VMEM((MAP, 3 * SPEC), BF16),
        taps=pltpu.VMEM((TAPS, C), F32),
        khat=pltpu.VMEM((SPEC, C), F32),
        spec=pltpu.VMEM((pairs, SPEC, 2 * C), F32),
        moved=pltpu.VMEM((pairs, MAP, 2 * C), F32),
        wave=pltpu.VMEM((3 * SPEC + MAP, 2 * C), BF16),
        conv=pltpu.VMEM((MAP, 2 * C), F32),
        n1=pltpu.VMEM((rows, C), F32),
        r1=pltpu.VMEM((rows, 1), F32),
        normed=pltpu.VMEM((rows, C), BF16),
        hidden=pltpu.VMEM((MAP // 2, FF // 2), F32),
        hidden_too=pltpu.VMEM((MAP // 2, FF // 2), F32),
        act=pltpu.VMEM((2, rows, FF // 2), BF16),
        slope=pltpu.VMEM((2, rows, FF // 2), F32),
        branch=pltpu.VMEM((rows, C), F32),
        n2=pltpu.VMEM((rows, C), F32),
        r2=pltpu.VMEM((rows, 1), F32),
        patches=pltpu.VMEM((own * CELLS, 4 * C), BF16),
        maps=pltpu.VMEM((own * CELLS, OUT), F32),
        back=pltpu.VMEM((own * CELLS, 4 * C), F32),
        rgrad=pltpu.VMEM((own, MAP, C), BF16),
        bgrad=pltpu.VMEM((rows, C), BF16),
        usum=pltpu.VMEM((32, C), F32),
        rows=pltpu.VMEM((8, C), F32),
        zhat=pltpu.VMEM((SPEC, C), F32),
        ghat=pltpu.VMEM((SPEC, 2 * C), F32),
        chigh=pltpu.VMEM((MAP, 2 * C), BF16),
        clow=pltpu.VMEM((MAP, 2 * C), BF16),
        grads=pltpu.VMEM((4, 4 * C, C), BF16),
        land=pltpu.VMEM((8, sum_rows, C), BF16),
        small=pltpu.VMEM((SMALL, C), F32),
        small_land=pltpu.VMEM((small_rows, C), F32),
        maps_out=pltpu.VMEM((ways, own * CELLS, OUT // ways), BF16),
        maps_in=pltpu.VMEM((ways, own * CELLS, OUT // ways), BF16),
        maps_held=pltpu.VMEM((ways, own * CELLS, -(-OUT // ways // 128) * 128), F32),
        image_out=pltpu.VMEM((ways, MAP, C), BF16),
        sum_send=pltpu.SemaphoreType.DMA((8, sum_copies)),
        sum_recv=pltpu.SemaphoreType.DMA((8, sum_copies)),
        small_send=pltpu.SemaphoreType.DMA((small_copies,)),
        small_recv=pltpu.SemaphoreType.DMA((small_copies,)),
        maps_send=pltpu.SemaphoreType.DMA((ways,)),
        maps_recv=pltpu.SemaphoreType.DMA((ways,)),
        image_send=pltpu.SemaphoreType.DMA((ways,)),
        image_recv=pltpu.SemaphoreType.DMA((ways,)),
    )


def landing(rows, least, steps):
    total, copies = 0, 0
    for at, bits in enumerate(steps):
        ways = 2**bits
        halving = rows % (ways * least) == 0 and at < len(steps) - 1
        rows = rows // ways if halving else rows
        total += (ways - 1) * rows
        copies += 2 * (ways - 1)
    return total, copies


class Sum:
    def __init__(self, work, land, total, rows, least, steps, sems):
        self.work, self.land, self.total = work, land, total
        self.steps, self.sems, self.least = steps, sems, least
        self.at, self.rows, self.start, self.used = 0, rows, 0, 0
        self.copies, self.path, self.slots, self.came = [], [], [], []
        self.count, self.halving, self.gathering = 0, True, False

    def send(self, source, target, axis, partner):
        copy = pltpu.make_async_remote_copy(
            src_ref=source,
            dst_ref=target,
            send_sem=self.sems[0].at[self.count],
            recv_sem=self.sems[1].at[self.count],
            device_id={axis: partner},
            device_id_type=pl.DeviceIdType.MESH,
        )
        copy.start()
        self.count += 1
        self.copies.append(copy)
        self.came.append(copy)

    def add(self, target, start, slots, rows):
        step = max(size for size in range(self.least, min(rows, 192) + 1, self.least) if rows % size == 0)

        def one(t, carry):
            to = pl.ds(pl.multiple_of(start + t * step, self.least), step)
            total = self.work[to, :]
            for slot in slots:
                total = total + self.land[pl.ds(pl.multiple_of(slot + t * step, self.least), step), :]
            target[to, :] = total
            return carry

        if rows == step:
            one(0, 0)
        else:
            lax.fori_loop(0, rows // step, one, 0)

    def reduce(self):
        start, rows, slots = self.start, self.rows, self.slots
        if self.came:
            for copy in self.came:
                copy.wait_recv()
            self.at += 1
            if self.at == len(self.steps):
                self.add(self.total, start, slots, rows)
                self.gather()
                return
            if not self.halving:
                for copy in self.came:
                    copy.wait_send()
                self.copies = self.copies[: len(self.copies) - len(self.came)]
        axis, index, bits = self.steps[self.at]
        ways = 2 ** len(bits)
        self.halving = rows % (ways * self.least) == 0 and self.at < len(self.steps) - 1
        count = rows // ways if self.halving else rows
        if slots and not self.halving:
            self.add(self.work, start, slots, rows)
        self.slots, self.came = [], []
        for mask in range(1, ways):
            partner, block = index, 0
            for k, (bit, delta) in enumerate(bits):
                away = mask >> k & 1
                partner = partner + away * delta
                block = block + (1 - bit if away else bit) * 2**k
            give = count * block if self.halving else 0
            if slots and self.halving:
                self.add(self.work, start + give, [slot + give for slot in slots], count)
            source = self.work.at[pl.ds(pl.multiple_of(start + give, self.least), count), :]
            self.send(source, self.land.at[pl.ds(self.used, count), :], axis, partner)
            self.slots.append(self.used)
            self.used += count
        keep = 0
        if self.halving:
            keep = count * sum(bit * 2**k for k, (bit, _) in enumerate(bits))
            at, size = start, rows
            for bit in reversed(bits):
                self.path.append((axis, index, [bit], at, size))
                size //= 2
                at = at + size * bit[0]
            if slots:
                self.add(self.work, start + keep, [slot + keep for slot in slots], count)
        self.start, self.rows = start + keep, count

    def gather(self):
        self.gathering, self.came = True, []
        if self.path:
            axis, index, bits, start, rows = self.path.pop()
            here = self.total.at[pl.ds(pl.multiple_of(self.start, self.least), self.rows), :]
            for mask in range(1, 2 ** len(bits)):
                partner = index
                for k, (_, delta) in enumerate(bits):
                    partner = partner + (mask >> k & 1) * delta
                self.send(here, here, axis, partner)
            self.start, self.rows = start, rows

    def go(self):
        if not self.gathering:
            self.reduce()
        elif self.came:
            for copy in self.came:
                copy.wait_recv()
            self.gather()

    def running(self):
        return not self.gathering or bool(self.came)

    def finish(self):
        for copy in self.copies:
            copy.wait_send()


PARTS = ((0, 0), (1, 0), (0, 768), (1, 768), (2, 0), (2, 768), (3, 0), (3, 768))
IMAGE, MAPS = 100, 101
SCHEDULE = {
    "p0": (1,),
    "m": (0,),
    "b": (1, 2),
    "j": (MAPS, 0, 3),
    "d0": (4,),
    "d1": (2,),
    "s3": (3, 1, 0, 5, 4),
    "u0": (2, 6),
    "u1": (1,),
    "n0": (0, 5),
    "l0": (7, 3),
    "l1": (6, 2),
    "l2": (4,),
    "l3": (0, 3, 5, 7),
    "l4": (1,),
    "l5": (4, 2),
    "i": (6,),
    "t": (8, 5, 0, 1, 3, 7, 8, 6, 4, 5, 0, 2, 3, 7, 1, 6, 8, 4, 5, 7, 2, 3, IMAGE, 6, 7),
    "end": (8, 1, 4, 5, 0, 2, 6, 7, 3, 1, 5, 4, 8, 0, 6, 7, 2, 5, 8, 3, 4, 6, 7),
}


def groups_of(groups, ways):
    left = groups.bit_length() - 1
    near = [1] if left else []
    left -= len(near)
    while left:
        near.append(min(2, left))
        left -= near[-1]
    return near, [1] * (ways.bit_length() - 1)


def routes(groups, ways):
    def steps(axis, sizes):
        index, stride, found = lax.axis_index(axis), 1, []
        for size in sizes:
            bits = []
            for _ in range(size):
                bit = lax.rem(lax.div(index, stride), 2)
                bits.append((bit, stride * (1 - 2 * bit)))
                stride *= 2
            found.append((axis, index, bits))
        return found

    near, far = groups_of(groups, ways)
    return steps("dp", near), steps("pipe", far)


def unpack_maps(own, ways, low, held, tall, cells):
    part, count = low.shape[2], own * ways

    def hold(t, carry):
        rows = pl.ds(pl.multiple_of(t * 16, 16), 16)
        for q in range(ways):
            held[q, rows, :part] = low[q, rows, :].astype(F32)
        return carry

    def unmap(a, carry):
        for lane in range(0, part, 128):
            for q in range(ways):
                for n in range(own):
                    v = held[q, pl.ds(pl.multiple_of((n * HALF + a) * 8, 8), 8), lane : lane + 128]
                    tall[pl.ds(lane // 128 * 8 * count + q * own + n, 8, stride=count), :] = v
            for b in range(HALF):
                at = lane // 128 * 8 * count + b * count
                v = tall[at : at + count, : min(128, part - lane)]
                cells[a, b, :, lane : min(lane + 128, part)] = v.astype(BF16)
        return carry

    lax.fori_loop(0, own * CELLS // 16, hold, 0)
    lax.fori_loop(0, HALF, unmap, 0)


def exchange(ways, source, land, sems):
    p = lax.axis_index("pipe")
    copies = []
    for j in range(1, ways):
        q = lax.rem(p + j, ways)
        copy = pltpu.make_async_remote_copy(
            src_ref=source.at[q],
            dst_ref=land.at[p],
            send_sem=sems[0].at[j - 1],
            recv_sem=sems[1].at[j - 1],
            device_id={"pipe": q},
            device_id_type=pl.DeviceIdType.MESH,
        )
        copy.start()
        copies.append(copy)
    return copies


def whole_kernel(own, ways, groups, *refs):
    keep = refs[0]
    ins = refs[1:12]
    images, out_grad, up, down, wpatch, from_cell, to_plain, to_taps, from_plain, to_cell = refs[12:22]
    total, maps_all, image_in, small_total = refs[22:26]
    s = SimpleNamespace(**dict(zip(scratch(own, ways, groups), refs[26:])))
    p = lax.axis_index("pipe")
    start = p * own
    fetched = {}
    for k, (name, source, target) in enumerate(
        (
            ("g", out_grad, s.og_in),
            ("x", images, s.x_in),
            ("f", from_plain, s.from_plain),
            ("e", to_cell, s.to_cell),
            ("u", up, s.up),
            ("d", down, s.down),
            ("w", wpatch, s.wpatch),
            ("c", from_cell, s.from_cell),
            ("p", to_plain, s.to_plain),
            ("t", to_taps, s.to_taps),
        )
    ):
        fetched[name] = pltpu.make_async_copy(source, target, s.in_sem.at[k])
        fetched[name].start()

    def keep_of(image):
        return keep[start + image].astype(F32) / 0.9

    near, far = routes(groups, ways)
    barrier = pltpu.get_barrier_semaphore()
    met = [("pipe", lax.rem(p + j, ways)) for j in range(1, ways)]
    for axis, index, bits in near:
        for mask in range(1, 2 ** len(bits)):
            met.append((axis, index + sum((mask >> k & 1) * delta for k, (_, delta) in enumerate(bits))))
    for axis, partner in met:
        pl.semaphore_signal(barrier, inc=1, device_id={axis: partner}, device_id_type=pl.DeviceIdType.MESH)

    steps = near + far
    turned = [(axis, index, bits[::-1]) for axis, index, bits in steps], steps

    def part_sum(i, k, first):
        rows = pl.ds(first, 2 * C)

        return Sum(
            s.grads.at[k, rows, :], s.land.at[i], total.at[k, rows, :], 2 * C, 16, turned[i % 2],
            (s.sum_send.at[i], s.sum_recv.at[i]),
        )

    sums = [part_sum(i, k, first) for i, (k, first) in enumerate(PARTS)]
    tail = Sum(
        s.small, s.small_land, small_total, SMALL, SMALL // 2, steps, (s.small_send, s.small_recv)
    )
    chains = sums + [tail]
    kept = {}
    needs = {"og": "g", "x": "x", "f": "fe", "up": "u", "down": "d", "p0": "w", "n": "cpt"}

    def at_point(name):
        for needed in needs.get(name, ""):
            fetched[needed].wait()
        if name == "p0":
            pl.semaphore_wait(barrier, len(met))
        if name == "l4":
            for copy in kept[MAPS]:
                copy.wait_recv()
            unpack_maps(own, ways, s.maps_in, s.maps_held, s.line, maps_all)
        for k in SCHEDULE.get(name, ()):
            if k == MAPS:
                kept[k] = exchange(ways, s.maps_out, s.maps_in, (s.maps_send, s.maps_recv))
                s.maps_in[p] = s.maps_out[p]
            elif k == IMAGE:
                kept[k] = exchange(ways, s.image_out, image_in, (s.image_send, s.image_recv))
                image_in[p] = s.image_out[p]
            else:
                chains[k].go()

    compute(own, start, keep_of, ins, s.grads, s.maps_out, s.image_out, s.small, s, at_point)
    at_point("end")
    while any(chain.running() for chain in chains):
        for chain in chains:
            if chain.running():
                chain.go()
    exchanged = kept[MAPS] + kept[IMAGE]
    for copy in kept[IMAGE]:
        copy.wait_recv()
    for copy in exchanged:
        copy.wait_send()
    for chain in chains:
        chain.finish()


def whole_call(own, ways, groups, args):
    vmem = pl.BlockSpec(memory_space=pltpu.VMEM)
    away = pl.BlockSpec(memory_space=pl.ANY)
    return pl.pallas_call(
        functools.partial(whole_kernel, own, ways, groups),
        out_shape=(
            pltpu.VMEM((4, 4 * C, C), BF16),
            pltpu.VMEM((HALF, HALF, own * ways, OUT // ways), BF16),
            pltpu.VMEM((ways, MAP, C), BF16),
            jax.ShapeDtypeStruct((SMALL, C), F32),
        ),
        in_specs=[pl.BlockSpec(memory_space=pltpu.SMEM)] + [vmem] * 11 + [away] * 10,
        out_specs=[vmem] * 4,
        scratch_shapes=list(scratch(own, ways, groups).values()),
        compiler_params=pltpu.CompilerParams(
            collective_id=0, has_side_effects=True, vmem_limit_bytes=57 * 2**20
        ),
    )(*args)


def finish_kernel(own, ways, grads, maps, image, small, *refs):
    (merged, image_grad, taps, kbias, gain1, shift1, up_grad, up_bias, down_grad, down_bias, scale, gain2,
     shift2, patch_grad, patch_bias, patches, downs, ups, images, tall, sems) = refs
    size, count = C // ways, own * ways

    def block(c):
        return pl.ds(c * C, C)

    sent = []

    def send(source, target):
        copy = pltpu.make_async_copy(source, target, sems.at[len(sent)])
        copy.start()
        sent.append(copy)

    def widen(k, c, target, row, lane):
        def step(t, carry):
            at = t * 32
            target[pl.ds(pl.multiple_of(row + at, 32), 32), lane : lane + C] = grads[
                k, pl.ds(pl.multiple_of(c * C + at, 32), 32), :
            ].astype(F32)
            return carry

        lax.fori_loop(0, C // 32, step, 0, unroll=4)

    def patch(c):
        widen(0, c, patches, c * C, 0)
        widen(1, c, patches, c * C, C)
        send(patches.at[block(c), :], patch_grad.at[block(c), :])

    send(maps, merged)

    def unpack(h, carry):
        for q in range(ways):
            v = image[q, pl.ds(pl.multiple_of(h * WIDE, WIDE), WIDE), :].astype(F32)
            for n in range(own):
                first = n * size // 128 * 128
                turn = v[:, first : min(first + 256, C)]
                if n * size > first:
                    turn = pltpu.roll(turn, turn.shape[1] - (n * size - first), 1)
                tall[pl.ds(q * own + n, WIDE, stride=count), :] = turn[:, :128]
        for w in range(SIDE):
            images[h, w] = tall[w * count : w * count + count, :size]
        return carry

    for c in range(2):
        patch(c)
        rows = pl.ds(c * HALF, HALF)
        lax.fori_loop(c * HALF, c * HALF + HALF, unpack, 0)
        send(images.at[rows], image_grad.at[rows])
    patch(2)
    patch(3)
    for c in range(4):
        widen(2, c, downs, c * C, 0)
        if c % 2:
            rows = pl.ds((c - 1) * C, 2 * C)
            send(downs.at[rows, :], down_grad.at[rows, :])
    for c in range(4):
        widen(3, c, ups, 0, c * C)
        if c % 2:
            lanes = pl.ds((c - 1) * C, 2 * C)
            send(ups.at[:, lanes], up_grad.at[:, lanes])
    for i in range(7):
        taps[i] = small[i * 8 : i * 8 + 7, :]
    for i, out in enumerate((kbias, gain1, shift1, down_bias, scale, gain2, shift2)):
        out[...] = small[i * 8 + 7 : i * 8 + 8, :].reshape(C)
    for k in range(4):
        up_bias[k * C : k * C + C] = small[TAPS + k : TAPS + k + 1, :].reshape(C)
    for k in range(2):
        patch_bias[k * C : k * C + C] = small[TAPS + 4 + k : TAPS + 5 + k, :].reshape(C)
    for copy in sent:
        copy.wait()


def finish_call(own, ways, grads, maps, image, small):
    count = ways * own
    size, part = C // ways, OUT // ways
    vector = jax.ShapeDtypeStruct((C,), F32)
    shapes = (
        jax.ShapeDtypeStruct((HALF, HALF, count, part), BF16),
        jax.ShapeDtypeStruct((SIDE, SIDE, count, size), F32),
        jax.ShapeDtypeStruct((7, 7, C), F32),
        vector,
        vector,
        vector,
        jax.ShapeDtypeStruct((C, FF), F32),
        jax.ShapeDtypeStruct((FF,), F32),
        jax.ShapeDtypeStruct((FF, C), F32),
        vector,
        vector,
        vector,
        vector,
        jax.ShapeDtypeStruct((4 * C, OUT), F32),
        jax.ShapeDtypeStruct((OUT,), F32),
    )
    away = pl.BlockSpec(memory_space=pl.ANY)
    near = pl.BlockSpec(memory_space=pltpu.VMEM)
    outs = pl.pallas_call(
        functools.partial(finish_kernel, own, ways),
        out_shape=shapes,
        in_specs=[near] * 4,
        out_specs=[away if k in (0, 1, 6, 8, 13) else near for k in range(15)],
        scratch_shapes=[
            pltpu.VMEM((4 * C, OUT), F32),
            pltpu.VMEM((FF, C), F32),
            pltpu.VMEM((C, FF), F32),
            pltpu.VMEM((SIDE, SIDE, count, size), F32),
            pltpu.VMEM((WIDE * count, 128), F32),
            pltpu.SemaphoreType.DMA((32,)),
        ],
        compiler_params=pltpu.CompilerParams(vmem_limit_bytes=50 * 2**20),
    )(*[pltpu.with_memory_space_constraint(v, pltpu.VMEM) for v in (grads, maps, image)], small)
    return (outs[0].transpose(2, 0, 1, 3), outs[1].transpose(2, 0, 1, 3)) + tuple(outs[2:])


def shards(
    images, depth_kernel, depth_bias, norm_gain, norm_shift, up_weight, up_bias, down_weight, down_bias,
    layer_scale, merge_gain, merge_shift, patch_weight, patch_bias, keep_mask, out_grad,
):
    ways = lax.axis_size("pipe")
    own = images.shape[0] // ways
    from_plain, from_cell, to_cell, to_plain, from_taps, to_taps = [jnp.asarray(m) for m in transforms()]
    packed = whole_call(
        own, ways, lax.axis_size("dp"),
        (keep_mask, depth_kernel, depth_bias, norm_gain, norm_shift, up_bias, down_bias, layer_scale,
         merge_gain, merge_shift, patch_bias, from_taps,
         images.transpose(1, 2, 0, 3), out_grad.transpose(1, 2, 0, 3), up_weight, down_weight, patch_weight,
         from_cell, to_plain, to_taps, from_plain, to_cell),
    )
    return finish_call(own, ways, *packed)


def solution(mesh):
    whole = P()
    split = P("dp")
    placed = (split,) + (whole,) * 13 + (split, split)
    owned = P("dp", None, None, "pipe")
    return jax.shard_map(
        shards, mesh=mesh, in_specs=placed, out_specs=(owned, owned) + (whole,) * 13, check_vma=False
    )
```
